32 devices in a mesh: group: 1, ep: 32 (over z, y, x, core).
Axes of the slice: x: 2, y: 2, z: 4, core: 2. Of those that a mesh axis runs over, the one named last changes fastest.
Arguments:
- queries: bfloat16 [128, 2, 128, 576], P(('group', 'ep')), may hold values from -16 to 16
- cache_pool: bfloat16 [2176, 64, 576], P(('group', 'ep')), may hold values from -16 to 16
- mig_block: int32 [32, 32], P(('group', 'ep')), may hold values from 0 to 68, as said below
- block_table: int32 [128, 17], P(('group', 'ep')), may hold values from 0 to 99, as said below
- lengths: int32 [128], P(('group', 'ep')), may hold values from 2 to 1088
- hidden_states: bfloat16 [256, 3584], P(('group', 'ep')), may hold values from -6 to 6
- routes: int32 [256, 2], P(('group', 'ep')), may hold values from 0 to 3, all different within a row; in each aligned block of 8 rows (0 to 7, 8 to 15, ...) at most 4 rows name the same one
- route_weight: bfloat16 [256, 2], P(('group', 'ep')), may hold values from 0.19921875 to 1
- w_gate: bfloat16 [32, 3584, 256], P('ep'), may hold values from -0.09375 to 0.09375
- w_up: bfloat16 [32, 3584, 256], P('ep'), may hold values from -0.09375 to 0.09375
- w_down: bfloat16 [32, 256, 3584], P('ep'), may hold values from -0.125 to 0.125
Outputs:
- attn_out: bfloat16 [128, 2, 128, 512], P(('group', 'ep'))
- moe_out: bfloat16 [256, 3584], P(('group', 'ep'))
The draws below stay inside these ranges and needn't reach their ends.
Inputs may be any that keep to these rules, and one draw needn't show every extreme that they name: `mig_block`: row s names, for each device d that receives a block from device s, the block of s that moves to d; every other entry, always including d = s, is 68; the blocks named in a row differ, and a row names at most 31 of them. `block_table`: entries below 68 name blocks that the request's device keeps (none that it sends away); 68 + s names the block that device s sends to it. On each device every kept block and every arriving block stands exactly once in its requests' tables, and each request's first entry is a kept block. `routes`: A token's 2 experts differ, and the rows of one device name every expert exactly 4 times.
All inputs are finite; a program needn't handle non-finite values.
Results may differ from the reference program's by a relative error of at most 0.0049.
Values may be sent and summed in bfloat16 or wider, within the bound.
A program may use at most 128 MiB of HBM per device.

```python
import math
import jax
import jax.numpy as jnp
import numpy as np
from jax import lax

D = 3584
H = 128
KVL = 512
LAT = 576
FF = 2048
FF_DEV = 256
SPLIT = 8
EXPERTS = 4
TOPK = 2
STEPS = 2
ROWS = 4
BLK = 64
MAXB = 17
NB = 68
MIG = 31
MAXLEN = 1088
MROWS = 8
CAP = 4
TOKENS = 128
MTOK = 256
POOL = 2176
N_EP = 32


def migration_plan(key):
    key = jax.random.fold_in(key, 101)
    key_off, key_lab, key_ids = jax.random.split(key, 3)
    offsets = jax.random.permutation(key_off, N_EP - 1)[:MIG] + 1
    labels = jax.random.permutation(key_lab, N_EP)
    anchor = jnp.arange(N_EP)
    source = jnp.broadcast_to(labels[anchor][:, None], (N_EP, MIG))
    target = labels[(anchor[:, None] + offsets[None, :]) % N_EP]
    id_keys = jax.random.split(key_ids, N_EP)
    picked = jax.vmap(lambda sub_key: jax.random.permutation(sub_key, NB)[:MIG])(id_keys)
    outline = jnp.full((N_EP, N_EP), NB, jnp.int32)
    return outline.at[source, target].set(picked.astype(jnp.int32))


def block_tables(key):
    outline = migration_plan(key)
    key = jax.random.fold_in(key, 202)
    key_pri, key_mix = jax.random.split(key)
    slot_count = NB + N_EP

    def one_device(device, pri_key, mix_key):
        sent_away = jnp.any(jnp.arange(NB)[:, None] == outline[device][None, :], axis=1)
        arriving = outline[:, device] < NB
        usable = jnp.concatenate([jnp.logical_not(sent_away), arriving])
        is_local = jnp.arange(slot_count) < NB
        priority = jax.random.permutation(pri_key, slot_count)
        ranking = priority + jnp.where(usable, jnp.where(is_local, 0, slot_count), 4 * slot_count)
        ordering = jnp.argsort(ranking, stable=True)[:NB]
        leaders = ordering[:ROWS]
        remainder = ordering[ROWS:][jax.random.permutation(mix_key, NB - ROWS)]
        return jnp.concatenate([leaders[:, None], remainder.reshape(ROWS, MAXB - 1)], axis=1)
    tables = jax.vmap(one_device)(jnp.arange(N_EP), jax.random.split(key_pri, N_EP), jax.random.split(key_mix, N_EP))
    return tables.reshape(N_EP * ROWS, MAXB).astype(jnp.int32)


def pool_values(key):
    key = jax.random.fold_in(key, 404)
    key_one = jax.random.fold_in(key, 0)
    drawn = jax.random.normal(key_one, (POOL, BLK, LAT), jnp.float32)
    return jnp.clip(drawn, -16.0, 16.0)


def draw_mig_block(key, part):
    return migration_plan(key)


def draw_block_table(key, part):
    return block_tables(key)


def draw_cache_pool(key, part):
    return pool_values(key).astype(jnp.bfloat16)


def draw_lengths(key, part):
    key = jax.random.fold_in(key, 303)
    key_one, key_two = jax.random.split(key)
    drawn = jax.random.randint(key_one, (N_EP * ROWS,), 2, MAXLEN + 1)
    position = jax.random.randint(key_two, (), 0, N_EP * ROWS)
    return jnp.where(jnp.arange(N_EP * ROWS) == position, MAXLEN, drawn).astype(jnp.int32)


def draw_queries(key, part):
    key = jax.random.fold_in(key, 505)
    key_one = jax.random.fold_in(key, 0)
    drawn = jax.random.normal(key_one, (TOKENS, STEPS, H, LAT), jnp.float32)
    return jnp.clip(drawn, -16.0, 16.0).astype(jnp.bfloat16)


def block_levels(stream_key, dims, cuts, least, top_value):
    level, own = 1.0, jax.random.fold_in(stream_key, 6)
    for dim, parts in cuts:
        heights = jnp.exp(jax.random.uniform(jax.random.fold_in(own, dim), (parts,), jnp.float32, least / len(cuts), top_value / len(cuts)))
        level = level * jnp.repeat(heights, dims[dim] // parts).reshape([-1 if axis == dim else 1 for axis in range(len(dims))])
    return level


def routed_block(rng, own, number, rows, count, top, reach, slope):
    order = jax.random.permutation(rng, count)
    crowded, ordinary = load_shares(count, rows * top, reach, slope, True), load_shares(count, rows * top, reach, slope, False)
    places = jnp.arange(count)

    def named(sizes, offset_by):
        used = int((sizes > 0).sum())
        fixed = max(1, used // 4)
        moved = fixed + (places - fixed + offset_by * (used - fixed)) % max(1, count - fixed)
        return jnp.zeros((count,), jnp.int32).at[order[jnp.where(places < fixed, places, moved)]].set(jnp.asarray(sizes, jnp.int32))

    sizes = jnp.where(number % 4 == 0, named(crowded, number // 4), named(ordinary, number - number // 4 - 1))
    mixed = jax.random.permutation(jax.random.fold_in(own, 3), count)
    donor, taker = mixed[0:count // 2 * 2:2], mixed[1:count // 2 * 2:2]
    room = jnp.minimum(sizes[donor] - 1, reach - sizes[taker]) // 2
    room = jnp.where((donor == order[0]) | (taker == order[0]) | (sizes[taker] == 0), 0, jnp.maximum(room, 0))
    moved = jax.random.randint(jax.random.fold_in(own, 4), (count // 2,), 0, 1 << 20) % (room + 1)
    sizes = sizes.at[donor].add(-moved).at[taker].add(moved)
    items = jnp.searchsorted(jnp.cumsum(sizes), jnp.arange(rows * top), side="right").astype(jnp.int32)
    grid = items.reshape(top, rows).T
    grid = grid[jax.random.permutation(jax.random.fold_in(own, 1), rows)]
    offset_by = jax.random.randint(jax.random.fold_in(own, 2), (rows, 1), 0, top)
    return jnp.take_along_axis(grid, (jnp.arange(top)[None, :] + offset_by) % top, axis=1)


def load_shares(count, total, most, lean, full):
    loads = [(1 << 20) // math.isqrt(grade ** lean) + 1 for grade in range(1, count + 1)]
    largest = most if full else min(most, max(-(-total // count), total * loads[0] // sum(loads)))
    least = 1 if total - largest >= count - 1 else 0
    counts, spare = [largest] + [least] * (count - 1), total - largest - least * (count - 1)
    while spare > 0:
        candidates = [i for i in range(1, count) if counts[i] < largest] or [i for i in range(1, count) if counts[i] < most]
        mass, budget = sum([loads[i] for i in candidates]), spare
        for i in candidates:
            extra = min(most - counts[i], max(1, budget * loads[i] // mass), spare)
            counts[i] = counts[i] + extra
            spare = spare - extra
    return np.array(counts)


def gaussian(rng, dims, scale, most, cuts=(), held_as=jnp.bfloat16):
    loudness = block_levels(rng, dims, cuts, -0.22, 0.18) if cuts else 1.0
    values = jax.random.normal(rng, dims, jnp.float32) * scale * loudness
    return jnp.minimum(jnp.maximum(values, -most), most).astype(held_as)


def setup_inputs(seed: int = 0, part: int = 0) -> dict:
    key_of = jax.random.split(jax.random.key(seed), 12)
    own_keys = jax.random.split(jax.random.fold_in(key_of[11], part), 12)
    queries = draw_queries(jax.random.fold_in(jax.random.fold_in(key_of[11], part), 71), part)
    cache_pool = draw_cache_pool(jax.random.fold_in(jax.random.fold_in(key_of[11], part), 71), part)
    mig_block = draw_mig_block(jax.random.fold_in(jax.random.fold_in(key_of[11], part), 71), part)
    block_table = draw_block_table(jax.random.fold_in(jax.random.fold_in(key_of[11], part), 71), part)
    lengths = draw_lengths(jax.random.fold_in(jax.random.fold_in(key_of[11], part), 71), part)
    hidden_states = gaussian(own_keys[5], (MTOK, D), 1.0, 6.0, ((0, 32),))
    routes_keys = jax.random.split(jax.random.fold_in(own_keys[6], 1), MTOK // MROWS)
    routes_turns = jax.random.permutation(jax.random.fold_in(own_keys[6], 3), MTOK // MROWS)
    routes = jax.vmap(lambda own, number: routed_block(jax.random.fold_in(own_keys[6], 2), own, number, MROWS, EXPERTS, TOPK, CAP, 0))(routes_keys, routes_turns).reshape((MTOK, TOPK))
    route_weight = jnp.clip(0.19921875 + 0.80078125 * jax.random.uniform(own_keys[7], (MTOK, TOPK), jnp.float32) ** block_levels(own_keys[7], (MTOK, TOPK), ((0, 32),), -0.2, 0.2), 0.19921875, 1.0).astype(jnp.bfloat16)
    w_gate = gaussian(key_of[8], (N_EP, D, FF_DEV), D ** -0.5, 0.09375, ((0, 32),))
    w_up = gaussian(key_of[9], (N_EP, D, FF_DEV), D ** -0.5, 0.09375, ((0, 32),))
    w_down = gaussian(key_of[10], (N_EP, FF_DEV, D), FF ** -0.5, 0.125, ((0, 32),))
    return {"queries": queries, "cache_pool": cache_pool, "mig_block": mig_block, "block_table": block_table, "lengths": lengths, "hidden_states": hidden_states, "routes": routes, "route_weight": route_weight, "w_gate": w_gate, "w_up": w_up, "w_down": w_down}


softmax_scale = 0.1353


def attend(queries, key_rows, lengths):
    scores = jnp.einsum("rshc,rtc->rsht", queries.astype(jnp.float32), key_rows.astype(jnp.float32)) * softmax_scale
    in_range = jnp.arange(key_rows.shape[1])[None, :] < lengths[:, None]
    scores = jnp.where(in_range[:, None, None, :], scores, -1e30)
    row_max = jnp.max(scores, axis=-1, keepdims=True)
    raised = jnp.exp(scores - row_max)
    probabilities = (raised / jnp.sum(raised, axis=-1, keepdims=True)).astype(jnp.bfloat16)
    values = key_rows[..., :KVL].astype(jnp.float32)
    return jnp.einsum("rsht,rtc->rshc", probabilities.astype(jnp.float32), values).astype(jnp.bfloat16)


def reference(queries, cache_pool, mig_block, block_table, lengths, hidden_states, routes, route_weight, w_gate, w_up, w_down):
    device = (jnp.arange(TOKENS, dtype=jnp.int32) // ROWS)[:, None]
    source = jnp.clip(block_table - NB, 0, N_EP - 1).astype(jnp.int32)
    moved_ids = mig_block[source, device].astype(jnp.int32)
    block_rows = jnp.where(block_table < NB, device * NB + block_table, source * NB + moved_ids).astype(jnp.int32)

    def per_device(packed_args):
        device_queries, device_rows, device_lengths = packed_args
        key_rows = cache_pool[device_rows].reshape(ROWS, MAXLEN, LAT)
        return attend(device_queries, key_rows, device_lengths)

    attn_out = lax.map(per_device, (queries.reshape(N_EP, ROWS, STEPS, H, LAT), block_rows.reshape(N_EP, ROWS, MAXB), lengths.reshape(N_EP, ROWS)))
    attn_out = attn_out.reshape(TOKENS, STEPS, H, KVL)

    def add_expert(expert, running):
        hits = routes == expert
        chosen = jnp.sum(hits.astype(jnp.int32), axis=1)
        weight = jnp.sum(jnp.where(hits, route_weight.astype(jnp.float32), 0.0), axis=1)
        picked = jnp.nonzero(chosen > 0, size=N_EP * CAP)[0].astype(jnp.int32)
        gate_matrix = jnp.transpose(lax.dynamic_slice_in_dim(w_gate, expert * SPLIT, SPLIT, 0), (1, 0, 2)).reshape(D, FF)
        up_matrix = jnp.transpose(lax.dynamic_slice_in_dim(w_up, expert * SPLIT, SPLIT, 0), (1, 0, 2)).reshape(D, FF)
        down_matrix = lax.dynamic_slice_in_dim(w_down, expert * SPLIT, SPLIT, 0).reshape(FF, D)
        rows_in = hidden_states[picked]
        gate_act = jnp.dot(rows_in, gate_matrix, preferred_element_type=jnp.float32)
        up_act = jnp.dot(rows_in, up_matrix, preferred_element_type=jnp.float32)
        activation = (jax.nn.silu(gate_act) * up_act).astype(jnp.bfloat16)
        expert_out = jnp.dot(activation, down_matrix, preferred_element_type=jnp.float32)
        return running.at[picked].add(weight[picked][:, None] * expert_out)

    moe_total = lax.fori_loop(0, EXPERTS, add_expert, jnp.zeros((MTOK, D), jnp.float32))
    return attn_out, moe_total.astype(jnp.bfloat16)
```

```python
import functools
import math

import jax
import jax.numpy as jnp
from jax import lax
from jax.experimental import pallas as pl
from jax.experimental.pallas import tpu as pltpu
from jax.sharding import PartitionSpec as P

KVL = 512
FF = 2048
SLOT = 4
QUARTERS = 4
LANES = 128
MESH = pl.DeviceIdType.MESH

softmax_scale = 0.1353


def send(src, dst, send_sem, recv_sem, target):
    return pltpu.make_async_remote_copy(
        src_ref=src,
        dst_ref=dst,
        send_sem=send_sem,
        recv_sem=recv_sem,
        device_id={"ep": target},
        device_id_type=MESH,
    )


def spread(quarter, rows, cols, transposed):
    shape = (cols, rows) if transposed else (rows, cols)
    flat = lax.broadcasted_iota(jnp.int32, shape, 1 if transposed else 0)
    wide = lax.broadcasted_iota(jnp.int32, shape, 0 if transposed else 1)
    match = flat + (flat >> 2) * 12 + quarter * SLOT == wide
    return jnp.where(match, 1.0, 0.0).astype(jnp.bfloat16)


def exchange_kernel(
    n,
    split,
    mig_ref,
    pool_ref,
    hidden_ref,
    pick_ref,
    combine_ref,
    gate_ref,
    up_ref,
    down_ref,
    arrived_ref,
    moe_ref,
    pool_v,
    outgoing,
    gate_v,
    up_v,
    down_v,
    token_out,
    token_in,
    gathered,
    part_out,
    part_in,
    back_out,
    back_in,
    load_sem,
    mig_send,
    mig_recv,
    token_send,
    token_recv,
    gather_send,
    gather_recv,
    part_send,
    part_recv,
    back_send,
    back_recv,
):
    me = lax.axis_index("ep")
    planes = n // split
    plane, place = me // split, me % split
    own_blocks = pool_ref.shape[0]
    width = hidden_ref.shape[1] // QUARTERS
    chunk = planes * SLOT
    wide = planes * SLOT * QUARTERS

    loads = [
        pltpu.make_async_copy(pool_ref, pool_v, load_sem.at[0]),
        pltpu.make_async_copy(gate_ref, gate_v, load_sem.at[1]),
        pltpu.make_async_copy(up_ref, up_v, load_sem.at[2]),
        pltpu.make_async_copy(down_ref, down_v, load_sem.at[3]),
    ]
    for load in loads:
        load.start()

    barrier = pltpu.get_barrier_semaphore()

    def greet(k, carry):
        pl.semaphore_signal(
            barrier, inc=1, device_id={"ep": (me + k) % n}, device_id_type=MESH
        )
        return carry

    lax.fori_loop(1, n, greet, 0)

    messages = jnp.zeros((wide, width), jnp.float32)
    for q in range(QUARTERS):
        messages += jnp.dot(
            pick_ref[q],
            hidden_ref[:, q * width : (q + 1) * width],
            preferred_element_type=jnp.float32,
        )
    token_out[...] = messages.astype(jnp.bfloat16).reshape(token_out.shape)
    token_in[plane] = token_out[plane]

    pl.semaphore_wait(barrier, n - 1)

    def token_copy(k):
        other = (plane + k) % planes
        return send(
            token_out.at[other],
            token_in.at[plane],
            token_send.at[k],
            token_recv.at[plane],
            other * split + place,
        )

    for k in range(1, planes):
        token_copy(k).start()

    loads[0].wait()

    def mig_copy(k):
        target = (me + k) % n
        return send(
            outgoing.at[k], arrived_ref.at[me], mig_send.at[k], mig_recv.at[me], target
        )

    def mig_start(k, carry):
        target = (me + k) % n
        block = jnp.minimum(mig_ref[0, target], own_blocks - 1)
        for c in range(KVL // LANES):
            outgoing[k, c * 64 : (c + 1) * 64, :] = pool_v[
                block, :, c * LANES : (c + 1) * LANES
            ]
        tail = pool_v[block, :, KVL:]
        outgoing[k, 256:288, :] = jnp.concatenate([tail[:32], tail[32:]], axis=1)
        mig_copy(k).start()
        return carry

    far = n - split
    lax.fori_loop(split, split + far // 2, mig_start, 0)

    for k in range(1, planes):
        other = (plane + k) % planes
        send(
            token_out.at[k], token_in.at[other], token_send.at[k], token_recv.at[other], me
        ).wait_recv()
    arrived_tokens = token_in[...].reshape(wide, width)
    for q in range(QUARTERS):
        gathered[place, :, q * width : (q + 1) * width] = jnp.dot(
            spread(q, chunk, wide, False),
            arrived_tokens,
            preferred_element_type=jnp.float32,
        ).astype(jnp.bfloat16)

    def gather_copy(k):
        other = (place + k) % split
        return send(
            gathered.at[place],
            gathered.at[place],
            gather_send.at[k],
            gather_recv.at[place],
            plane * split + other,
        )

    for k in range(1, split):
        gather_copy(k).start()

    lax.fori_loop(split + far // 2, n, mig_start, 0)

    for load in loads[1:]:
        load.wait()
    for k in range(1, split):
        other = (place + k) % split
        send(
            gathered.at[place],
            gathered.at[other],
            gather_send.at[k],
            gather_recv.at[other],
            me,
        ).wait_recv()

    rows = gathered[...].reshape(split * chunk, gathered.shape[2])
    gate_act = jnp.dot(rows, gate_v[0], preferred_element_type=jnp.float32)
    up_act = jnp.dot(rows, up_v[0], preferred_element_type=jnp.float32)
    activation = (gate_act / (1.0 + jnp.exp(-gate_act)) * up_act).astype(jnp.bfloat16)
    for q in range(QUARTERS):
        columns = slice(q * width, (q + 1) * width)
        part_out[:, :, columns] = (
            jnp.dot(activation, down_v[0, :, columns], preferred_element_type=jnp.float32)
            .astype(jnp.bfloat16)
            .reshape(split, chunk, width)
        )

    def part_copy(k):
        other = (place + k) % split
        return send(
            part_out.at[other],
            part_in.at[place],
            part_send.at[k],
            part_recv.at[place],
            plane * split + other,
        )

    for k in range(1, split):
        part_copy(k).start()
    part_in[place] = part_out[place]

    lax.fori_loop(1, split, mig_start, 0)

    for k in range(1, split):
        other = (place + k) % split
        send(
            part_out.at[other], part_in.at[other], part_send.at[k], part_recv.at[other], me
        ).wait_recv()
    messages = jnp.zeros((wide, width), jnp.float32)
    for q in range(QUARTERS):
        columns = slice(q * width, (q + 1) * width)
        total = part_in[0, :, columns].astype(jnp.float32)
        for p in range(1, split):
            total += part_in[p, :, columns].astype(jnp.float32)
        messages += jnp.dot(
            spread(q, chunk, wide, True),
            total.astype(jnp.bfloat16),
            preferred_element_type=jnp.float32,
        )
    back_out[...] = messages.astype(jnp.bfloat16).reshape(back_out.shape)
    back_in[plane] = back_out[plane]

    def back_copy(k):
        other = (plane + k) % planes
        return send(
            back_out.at[other],
            back_in.at[plane],
            back_send.at[k],
            back_recv.at[plane],
            other * split + place,
        )

    for k in range(1, planes):
        back_copy(k).start()
    for k in range(1, planes):
        other = (plane + k) % planes
        send(
            back_out.at[k], back_in.at[other], back_send.at[k], back_recv.at[other], me
        ).wait_recv()
    returned = back_in[...].reshape(wide, width)
    for q in range(QUARTERS):
        moe_ref[:, q * width : (q + 1) * width] = jnp.dot(
            combine_ref[q], returned, preferred_element_type=jnp.float32
        ).astype(jnp.bfloat16)

    for k in range(1, planes):
        token_copy(k).wait_send()
        back_copy(k).wait_send()
    for k in range(1, split):
        gather_copy(k).wait_send()
        part_copy(k).wait_send()

    def mig_wait(k, carry):
        source = (me + k) % n
        send(
            outgoing.at[k], arrived_ref.at[source], mig_send.at[k], mig_recv.at[source], me
        ).wait_recv()
        mig_copy(k).wait_send()
        return carry

    lax.fori_loop(1, n, mig_wait, 0)


def exchange(cache_pool, mig_block, hidden_states, pick, combine, w_gate, w_up, w_down, n, split):
    blocks, positions, entries = cache_pool.shape
    tokens, model_width = hidden_states.shape
    packed = positions * entries // LANES
    planes = n // split
    chunk = planes * SLOT
    width = model_width // QUARTERS
    any_space = pl.BlockSpec(memory_space=pl.ANY)
    vmem = pl.BlockSpec(memory_space=pltpu.VMEM)
    bf16 = jnp.bfloat16
    dma = pltpu.SemaphoreType.DMA
    return pl.pallas_call(
        functools.partial(exchange_kernel, n, split),
        out_shape=(
            jax.ShapeDtypeStruct((n, packed, LANES), bf16),
            jax.ShapeDtypeStruct((tokens, model_width), bf16),
        ),
        in_specs=[
            pl.BlockSpec(memory_space=pltpu.SMEM),
            any_space,
            vmem,
            vmem,
            vmem,
            any_space,
            any_space,
            any_space,
        ],
        out_specs=(any_space, vmem),
        scratch_shapes=[
            pltpu.VMEM(cache_pool.shape, bf16),
            pltpu.VMEM((n, packed, LANES), bf16),
            pltpu.VMEM(w_gate.shape, bf16),
            pltpu.VMEM(w_up.shape, bf16),
            pltpu.VMEM(w_down.shape, bf16),
            pltpu.VMEM((planes, SLOT * QUARTERS, width), bf16),
            pltpu.VMEM((planes, SLOT * QUARTERS, width), bf16),
            pltpu.VMEM((split, chunk, model_width), bf16),
            pltpu.VMEM((split, chunk, model_width), bf16),
            pltpu.VMEM((split, chunk, model_width), bf16),
            pltpu.VMEM((planes, SLOT * QUARTERS, width), bf16),
            pltpu.VMEM((planes, SLOT * QUARTERS, width), bf16),
            dma((4,)),
            dma((n,)),
            dma((n,)),
            dma((planes,)),
            dma((planes,)),
            dma((split,)),
            dma((split,)),
            dma((split,)),
            dma((split,)),
            dma((planes,)),
            dma((planes,)),
        ],
        compiler_params=pltpu.CompilerParams(
            collective_id=0, has_side_effects=True, vmem_limit_bytes=48 * 1024 * 1024
        ),
        name="exchange",
    )(mig_block, cache_pool, hidden_states, pick, combine, w_gate, w_up, w_down)


def attend_kernel(sizes, table_ref, lengths_ref, queries_ref, pool_ref, arrived_ref, out_ref, keys):
    request = pl.program_id(0)
    own_blocks, positions, entries = pool_ref.shape
    length = lengths_ref[request]
    used = (length + positions - 1) // positions

    @pl.when(request == 0)
    def _():
        keys[...] = jnp.zeros_like(keys)

    def place_block(b, carry):
        entry = table_ref[request, b]
        start = pl.multiple_of(b * positions, positions)

        @pl.when(entry < own_blocks)
        def _():
            keys[pl.ds(start, positions), :] = pool_ref[entry]

        @pl.when(entry >= own_blocks)
        def _():
            source = entry - own_blocks
            for c in range(KVL // LANES):
                keys[pl.ds(start, positions), c * LANES : (c + 1) * LANES] = arrived_ref[
                    source, c * positions : (c + 1) * positions, :
                ]
            tail = arrived_ref[source, 256:288, :]
            keys[pl.ds(start, 32), KVL:] = tail[:, :64]
            keys[pl.ds(start + 32, 32), KVL:] = tail[:, 64:]

        return carry

    lax.fori_loop(0, used, place_block, 0)
    steps, heads = queries_ref.shape[1], queries_ref.shape[2]
    queries = queries_ref[0].reshape(steps * heads, entries)

    def attend(count):
        rows = count * positions
        scores = lax.dot_general(
            queries,
            keys[:rows, :],
            (((1,), (1,)), ((), ())),
            preferred_element_type=jnp.float32,
        ) * (softmax_scale * math.log2(math.e))
        where = lax.broadcasted_iota(jnp.int32, scores.shape, 1)
        scores = jnp.where(where < length, scores, -1e30)
        raised = jnp.exp2(scores - jnp.max(scores, axis=1, keepdims=True))
        total = jnp.sum(raised, axis=1, keepdims=True)
        out = jnp.dot(
            raised.astype(jnp.bfloat16), keys[:rows, :KVL], preferred_element_type=jnp.float32
        )
        out_ref[0] = (out / total).astype(jnp.bfloat16).reshape(steps, heads, KVL)

    low = 0
    for count in sizes:

        @pl.when((used > low) & (used <= count))
        def _():
            attend(count)

        low = count


def attention(queries, cache_pool, arrived, block_table, lengths):
    requests, steps, heads, entries = queries.shape
    blocks = block_table.shape[1]
    sizes = tuple(c for c in (4, 8, 12) if c < blocks) + (blocks,)
    smem = pl.BlockSpec(memory_space=pltpu.SMEM)
    vmem = pl.BlockSpec(memory_space=pltpu.VMEM)
    return pl.pallas_call(
        functools.partial(attend_kernel, sizes),
        grid=(requests,),
        out_shape=jax.ShapeDtypeStruct((requests, steps, heads, KVL), jnp.bfloat16),
        in_specs=[
            smem,
            smem,
            pl.BlockSpec((1, steps, heads, entries), lambda r: (r, 0, 0, 0)),
            vmem,
            vmem,
        ],
        out_specs=pl.BlockSpec((1, steps, heads, KVL), lambda r: (r, 0, 0, 0)),
        scratch_shapes=[pltpu.VMEM((blocks * cache_pool.shape[1], entries), jnp.bfloat16)],
        compiler_params=pltpu.CompilerParams(vmem_limit_bytes=48 * 1024 * 1024),
        name="attention",
    )(block_table, lengths, queries, cache_pool, arrived)


def local(
    queries,
    cache_pool,
    mig_block,
    block_table,
    lengths,
    hidden_states,
    routes,
    route_weight,
    w_gate,
    w_up,
    w_down,
):
    n = lax.axis_size("ep")
    split = FF // w_gate.shape[2]
    experts = n // split
    tokens = hidden_states.shape[0]
    ids = jnp.arange(experts, dtype=jnp.int32)
    matches = routes[:, :, None] == ids[None, None, :]
    hit = jnp.any(matches, axis=1)
    weight = jnp.sum(jnp.where(matches, route_weight[:, :, None], jnp.zeros((), jnp.bfloat16)), axis=1)
    order = jnp.arange(tokens)
    earlier = order[None, :] < order[:, None]
    rank = jnp.sum((earlier[:, :, None] & hit[None, :, :]).astype(jnp.int32), axis=1)
    slots = jnp.arange(SLOT)
    chosen = hit[:, :, None] & (rank[:, :, None] == slots)
    quarters = jnp.arange(QUARTERS)
    same = quarters[:, None] == quarters[None, :]
    wide = experts * QUARTERS * SLOT
    both = same[:, None, None, :, None] & chosen[None, :, :, None, :]
    combine = jnp.where(
        both, weight[None, :, :, None, None], jnp.zeros((), jnp.bfloat16)
    ).reshape(QUARTERS, tokens, wide)
    pick = both.astype(jnp.bfloat16).reshape(QUARTERS, tokens, wide).swapaxes(1, 2)
    arrived, moe_out = exchange(
        cache_pool, mig_block, hidden_states, pick, combine, w_gate, w_up, w_down, n, split
    )
    attn_out = attention(queries, cache_pool, arrived, block_table, lengths)
    return attn_out, moe_out


def solution(mesh):
    placed = (
        P(("group", "ep"), None, None, None),
        P(("group", "ep"), None, None),
        P(("group", "ep"), None),
        P(("group", "ep"), None),
        P(("group", "ep")),
        P(("group", "ep"), None),
        P(("group", "ep"), None),
        P(("group", "ep"), None),
        P("ep", None, None),
        P("ep", None, None),
        P("ep", None, None),
    )
    return jax.shard_map(
        local,
        mesh=mesh,
        in_specs=placed,
        out_specs=(P(("group", "ep"), None, None, None), P(("group", "ep"), None)),
        check_vma=False,
    )
```

```python
import functools
import math

import jax
import jax.numpy as jnp
from jax import lax
from jax.experimental import pallas as pl
from jax.experimental.pallas import tpu as pltpu
from jax.sharding import PartitionSpec as P

KVL = 512
FF = 2048
SLOT = 4
QUARTERS = 4
LANES = 128
MESH = pl.DeviceIdType.MESH

softmax_scale = 0.1353
score_factor = softmax_scale * math.log2(math.e)
W1, W2 = 4, 12


def send(src, dst, send_sem, recv_sem, target):
    return pltpu.make_async_remote_copy(
        src_ref=src,
        dst_ref=dst,
        send_sem=send_sem,
        recv_sem=recv_sem,
        device_id={"ep": target},
        device_id_type=MESH,
    )


def spread(quarter, rows, cols, transposed):
    shape = (cols, rows) if transposed else (rows, cols)
    flat = lax.broadcasted_iota(jnp.int32, shape, 1 if transposed else 0)
    wide = lax.broadcasted_iota(jnp.int32, shape, 0 if transposed else 1)
    match = flat + (flat >> 2) * 12 + quarter * SLOT == wide
    return jnp.where(match, 1.0, 0.0).astype(jnp.bfloat16)


def exchange_kernel(
    n,
    split,
    mig_ref,
    pool_ref,
    hidden_ref,
    pick_ref,
    combine_ref,
    gate_ref,
    up_ref,
    down_ref,
    table_ref,
    lengths_ref,
    queries_ref,
    arrived_ref,
    moe_ref,
    rows_ref,
    partial_ref,
    stats_ref,
    pool_v,
    outgoing,
    gate_v,
    up_v,
    down_v,
    token_out,
    token_in,
    gathered,
    part_out,
    part_in,
    back_out,
    back_in,
    queries_v,
    rows_v,
    keys,
    bias,
    partial_v,
    stats_v,
    load_sem,
    mig_send,
    mig_recv,
    token_send,
    token_recv,
    gather_send,
    gather_recv,
    part_send,
    part_recv,
    back_send,
    back_recv,
    store_sem,
):
    me = lax.axis_index("ep")
    planes = n // split
    plane, place = me // split, me % split
    own_blocks = pool_ref.shape[0]
    width = hidden_ref.shape[1] // QUARTERS
    chunk = planes * SLOT
    wide = planes * SLOT * QUARTERS

    loads = [
        pltpu.make_async_copy(pool_ref, pool_v, load_sem.at[0]),
        pltpu.make_async_copy(gate_ref, gate_v, load_sem.at[1]),
        pltpu.make_async_copy(up_ref, up_v, load_sem.at[2]),
        pltpu.make_async_copy(down_ref, down_v, load_sem.at[3]),
        pltpu.make_async_copy(queries_ref, queries_v, load_sem.at[4]),
    ]
    for load in loads:
        load.start()

    barrier = pltpu.get_barrier_semaphore()

    def greet(k, carry):
        pl.semaphore_signal(
            barrier, inc=1, device_id={"ep": (me + k) % n}, device_id_type=MESH
        )
        return carry

    lax.fori_loop(1, n, greet, 0)

    messages = jnp.zeros((wide, width), jnp.float32)
    for q in range(QUARTERS):
        messages += jnp.dot(
            pick_ref[q],
            hidden_ref[:, q * width : (q + 1) * width],
            preferred_element_type=jnp.float32,
        )
    token_out[...] = messages.astype(jnp.bfloat16).reshape(token_out.shape)
    token_in[plane] = token_out[plane]

    pl.semaphore_wait(barrier, n - 1)

    def token_copy(k):
        other = (plane + k) % planes
        return send(
            token_out.at[other],
            token_in.at[plane],
            token_send.at[k],
            token_recv.at[plane],
            other * split + place,
        )

    for k in range(1, planes):
        token_copy(k).start()

    loads[0].wait()

    def partner(k):
        flips = n - (k * 11) % n
        result = me
        for bit in range(n.bit_length() - 1):
            power = 2**bit
            flip = (flips // power) % 2
            held = (me // power) % 2
            result = result + flip * (1 - 2 * held) * power
        return result

    def mig_copy(k):
        return send(
            outgoing.at[k], arrived_ref.at[me], mig_send.at[k], mig_recv.at[me], partner(k)
        )

    def mig_start(k, carry):
        target = partner(k)
        block = jnp.minimum(mig_ref[0, target], own_blocks - 1)
        for c in range(KVL // LANES):
            outgoing[k, c * 64 : (c + 1) * 64, :] = pool_v[
                block, :, c * LANES : (c + 1) * LANES
            ]
        tail = pool_v[block, :, KVL:]
        outgoing[k, 256:288, :] = jnp.concatenate([tail[:32], tail[32:]], axis=1)
        mig_copy(k).start()
        return carry

    requests, blocks = table_ref.shape
    positions = pool_ref.shape[1]
    steps = queries_ref.shape[1]
    heads = queries_ref.shape[3]

    def kept_part(request, carry):
        length = lengths_ref[request]
        lane = lax.broadcasted_iota(jnp.int32, (1, positions), 1)
        for b in range(blocks):
            entry = table_ref[request, b]
            span = slice(b * positions, (b + 1) * positions)
            keys[span, :] = pool_v[jnp.minimum(entry, own_blocks - 1)]
            limit = jnp.where(entry < own_blocks, length - b * positions, 0)
            bias[:, span] = jnp.where(lane < limit, 0.0, -1e30)
        for step in range(steps):
            rows_v[request, step * heads : (step + 1) * heads, :] = queries_v[request, step].T
        scores = (
            lax.dot_general(
                rows_v[request],
                keys[...],
                (((1,), (1,)), ((), ())),
                preferred_element_type=jnp.float32,
            )
            * score_factor
            + bias[...]
        )
        row_max = jnp.max(scores, axis=1, keepdims=True)
        raised = jnp.exp2(scores - row_max)
        total = jnp.sum(raised, axis=1, keepdims=True)
        partial_v[request] = jnp.dot(
            raised.astype(jnp.bfloat16), keys[:, :KVL], preferred_element_type=jnp.float32
        )
        lane = lax.broadcasted_iota(jnp.int32, (steps * heads, LANES), 1)
        stats_v[request] = jnp.where(lane == 0, row_max, total)
        return carry

    stores = [
        pltpu.make_async_copy(rows_v, rows_ref, store_sem.at[0]),
        pltpu.make_async_copy(partial_v, partial_ref, store_sem.at[1]),
        pltpu.make_async_copy(stats_v, stats_ref, store_sem.at[2]),
    ]

    first, second = 1 + (n - 1) * W1 // 31, 1 + (n - 1) * W2 // 31
    lax.fori_loop(1, first, mig_start, 0)

    for k in range(1, planes):
        other = (plane + k) % planes
        send(
            token_out.at[k], token_in.at[other], token_send.at[k], token_recv.at[other], me
        ).wait_recv()
    arrived_tokens = token_in[...].reshape(wide, width)
    for q in range(QUARTERS):
        gathered[place, :, q * width : (q + 1) * width] = jnp.dot(
            spread(q, chunk, wide, False),
            arrived_tokens,
            preferred_element_type=jnp.float32,
        ).astype(jnp.bfloat16)

    def gather_copy(k):
        other = (place + k) % split
        return send(
            gathered.at[place],
            gathered.at[place],
            gather_send.at[k],
            gather_recv.at[place],
            plane * split + other,
        )

    for k in range(1, split):
        gather_copy(k).start()

    lax.fori_loop(first, second, mig_start, 0)

    for load in loads[1:]:
        load.wait()
    lax.fori_loop(0, requests // 2, kept_part, 0)
    for k in range(1, split):
        other = (place + k) % split
        send(
            gathered.at[place],
            gathered.at[other],
            gather_send.at[k],
            gather_recv.at[other],
            me,
        ).wait_recv()

    rows = gathered[...].reshape(split * chunk, gathered.shape[2])
    gate_act = jnp.dot(rows, gate_v[0], preferred_element_type=jnp.float32)
    up_act = jnp.dot(rows, up_v[0], preferred_element_type=jnp.float32)
    activation = (gate_act / (1.0 + jnp.exp(-gate_act)) * up_act).astype(jnp.bfloat16)
    for q in range(QUARTERS):
        columns = slice(q * width, (q + 1) * width)
        part_out[:, :, columns] = (
            jnp.dot(activation, down_v[0, :, columns], preferred_element_type=jnp.float32)
            .astype(jnp.bfloat16)
            .reshape(split, chunk, width)
        )

    def part_copy(k):
        other = (place + k) % split
        return send(
            part_out.at[other],
            part_in.at[place],
            part_send.at[k],
            part_recv.at[place],
            plane * split + other,
        )

    for k in range(1, split):
        part_copy(k).start()
    part_in[place] = part_out[place]

    lax.fori_loop(second, n, mig_start, 0)
    lax.fori_loop(requests // 2, requests, kept_part, 0)
    for store in stores:
        store.start()

    for k in range(1, split):
        other = (place + k) % split
        send(
            part_out.at[other], part_in.at[other], part_send.at[k], part_recv.at[other], me
        ).wait_recv()
    messages = jnp.zeros((wide, width), jnp.float32)
    for q in range(QUARTERS):
        columns = slice(q * width, (q + 1) * width)
        total = part_in[0, :, columns].astype(jnp.float32)
        for p in range(1, split):
            total += part_in[p, :, columns].astype(jnp.float32)
        messages += jnp.dot(
            spread(q, chunk, wide, True),
            total.astype(jnp.bfloat16),
            preferred_element_type=jnp.float32,
        )
    back_out[...] = messages.astype(jnp.bfloat16).reshape(back_out.shape)
    back_in[plane] = back_out[plane]

    def back_copy(k):
        other = (plane + k) % planes
        return send(
            back_out.at[other],
            back_in.at[plane],
            back_send.at[k],
            back_recv.at[plane],
            other * split + place,
        )

    for k in range(1, planes):
        back_copy(k).start()
    for k in range(1, planes):
        other = (plane + k) % planes
        send(
            back_out.at[k], back_in.at[other], back_send.at[k], back_recv.at[other], me
        ).wait_recv()
    returned = back_in[...].reshape(wide, width)
    for q in range(QUARTERS):
        moe_ref[:, q * width : (q + 1) * width] = jnp.dot(
            combine_ref[q], returned, preferred_element_type=jnp.float32
        ).astype(jnp.bfloat16)

    for k in range(1, planes):
        token_copy(k).wait_send()
        back_copy(k).wait_send()
    for k in range(1, split):
        gather_copy(k).wait_send()
        part_copy(k).wait_send()

    def mig_wait(k, carry):
        source = partner(k)
        send(
            outgoing.at[k], arrived_ref.at[source], mig_send.at[k], mig_recv.at[source], me
        ).wait_recv()
        mig_copy(k).wait_send()
        return carry

    for store in stores:
        store.wait()
    lax.fori_loop(1, n, mig_wait, 0)


def exchange(
    cache_pool,
    mig_block,
    hidden_states,
    pick,
    combine,
    w_gate,
    w_up,
    w_down,
    block_table,
    lengths,
    queries,
    n,
    split,
):
    blocks, positions, entries = cache_pool.shape
    tokens, model_width = hidden_states.shape
    packed = positions * entries // LANES
    requests, steps, _, heads = queries.shape
    height = steps * heads
    length = block_table.shape[1] * positions
    planes = n // split
    chunk = planes * SLOT
    width = model_width // QUARTERS
    any_space = pl.BlockSpec(memory_space=pl.ANY)
    vmem = pl.BlockSpec(memory_space=pltpu.VMEM)
    smem = pl.BlockSpec(memory_space=pltpu.SMEM)
    bf16 = jnp.bfloat16
    dma = pltpu.SemaphoreType.DMA
    return pl.pallas_call(
        functools.partial(exchange_kernel, n, split),
        out_shape=(
            jax.ShapeDtypeStruct((n, packed, LANES), bf16),
            jax.ShapeDtypeStruct((tokens, model_width), bf16),
            jax.ShapeDtypeStruct((requests, height, entries), bf16),
            jax.ShapeDtypeStruct((requests, height, KVL), jnp.float32),
            jax.ShapeDtypeStruct((requests, height, LANES), jnp.float32),
        ),
        in_specs=[
            smem,
            any_space,
            vmem,
            vmem,
            vmem,
            any_space,
            any_space,
            any_space,
            smem,
            smem,
            any_space,
        ],
        out_specs=(any_space, vmem, any_space, any_space, any_space),
        scratch_shapes=[
            pltpu.VMEM(cache_pool.shape, bf16),
            pltpu.VMEM((n, packed, LANES), bf16),
            pltpu.VMEM(w_gate.shape, bf16),
            pltpu.VMEM(w_up.shape, bf16),
            pltpu.VMEM(w_down.shape, bf16),
            pltpu.VMEM((planes, SLOT * QUARTERS, width), bf16),
            pltpu.VMEM((planes, SLOT * QUARTERS, width), bf16),
            pltpu.VMEM((split, chunk, model_width), bf16),
            pltpu.VMEM((split, chunk, model_width), bf16),
            pltpu.VMEM((split, chunk, model_width), bf16),
            pltpu.VMEM((planes, SLOT * QUARTERS, width), bf16),
            pltpu.VMEM((planes, SLOT * QUARTERS, width), bf16),
            pltpu.VMEM(queries.shape, bf16),
            pltpu.VMEM((requests, height, entries), bf16),
            pltpu.VMEM((length, entries), bf16),
            pltpu.VMEM((1, length), jnp.float32),
            pltpu.VMEM((requests, height, KVL), jnp.float32),
            pltpu.VMEM((requests, height, LANES), jnp.float32),
            dma((5,)),
            dma((n,)),
            dma((n,)),
            dma((planes,)),
            dma((planes,)),
            dma((split,)),
            dma((split,)),
            dma((split,)),
            dma((split,)),
            dma((planes,)),
            dma((planes,)),
            dma((3,)),
        ],
        compiler_params=pltpu.CompilerParams(
            collective_id=0, has_side_effects=True, vmem_limit_bytes=60 * 1024 * 1024
        ),
        name="exchange",
    )(
        mig_block,
        cache_pool,
        hidden_states,
        pick,
        combine,
        w_gate,
        w_up,
        w_down,
        block_table,
        lengths,
        queries,
    )


def attend_kernel(
    own_blocks,
    positions,
    sizes,
    table_ref,
    lengths_ref,
    rows_ref,
    partial_ref,
    stats_ref,
    arrived_ref,
    out_ref,
    fetched,
    keys,
    sem,
):
    request = pl.program_id(0)
    steps, heads = out_ref.shape[1], out_ref.shape[2]
    length = lengths_ref[request]

    def fetch(source):
        return pltpu.make_async_copy(
            arrived_ref.at[source], fetched.at[source], sem.at[source]
        )

    def used_blocks(row):
        return (lengths_ref[row] + positions - 1) // positions

    used = used_blocks(request)

    @pl.when(request == 0)
    def _():
        for row in range(table_ref.shape[0]):

            def begin(b, carry):
                entry = table_ref[row, b]

                @pl.when(entry >= own_blocks)
                def _():
                    fetch(entry - own_blocks).start()

                return carry

            lax.fori_loop(0, used_blocks(row), begin, 0)
        keys[...] = jnp.zeros_like(keys)

    def place_block(b, count):
        entry = table_ref[request, b]
        moved = entry >= own_blocks

        @pl.when(moved)
        def _():
            source = entry - own_blocks
            fetch(source).wait()
            start = pl.multiple_of(count * positions, positions)
            half = positions // 2
            for c in range(KVL // LANES):
                keys[pl.ds(start, positions), c * LANES : (c + 1) * LANES] = fetched[
                    source, c * positions : (c + 1) * positions, :
                ]
            tail = fetched[source, KVL // LANES * positions :, :]
            keys[pl.ds(start, half), KVL:] = tail[:, :64]
            keys[pl.ds(start + half, half), KVL:] = tail[:, 64:]

        return count + moved.astype(jnp.int32)

    count = lax.fori_loop(0, used, place_block, 0)
    last_moved = table_ref[request, used - 1] >= own_blocks
    limit = count * positions - jnp.where(last_moved, used * positions - length, 0)
    old_max = stats_ref[0, :, 0:1]
    old_total = stats_ref[0, :, 1:2]

    @pl.when(count == 0)
    def _():
        out_ref[0] = (partial_ref[0] / old_total).astype(jnp.bfloat16).reshape(steps, heads, KVL)

    def attend(size):
        rows = size * positions
        scores = (
            lax.dot_general(
                rows_ref[0],
                keys[:rows, :],
                (((1,), (1,)), ((), ())),
                preferred_element_type=jnp.float32,
            )
            * score_factor
        )
        where = lax.broadcasted_iota(jnp.int32, scores.shape, 1)
        scores = jnp.where(where < limit, scores, -1e30)
        row_max = jnp.maximum(jnp.max(scores, axis=1, keepdims=True), old_max)
        raised = jnp.exp2(scores - row_max)
        keep = jnp.exp2(old_max - row_max)
        total = jnp.sum(raised, axis=1, keepdims=True) + keep * old_total
        out = keep * partial_ref[0] + jnp.dot(
            raised.astype(jnp.bfloat16), keys[:rows, :KVL], preferred_element_type=jnp.float32
        )
        out_ref[0] = (out / total).astype(jnp.bfloat16).reshape(steps, heads, KVL)

    low = 0
    for size in sizes:

        @pl.when((count > low) & (count <= size))
        def _():
            attend(size)

        low = size


def attention(block_table, lengths, rows, partial, stats, arrived, own_blocks, positions, steps):
    requests, height, entries = rows.shape
    blocks = block_table.shape[1]
    sizes = tuple(c for c in (4, 8, 12) if c < blocks) + (blocks,)
    smem = pl.BlockSpec(memory_space=pltpu.SMEM)
    heads = height // steps
    return pl.pallas_call(
        functools.partial(attend_kernel, own_blocks, positions, sizes),
        grid=(requests,),
        out_shape=jax.ShapeDtypeStruct((requests, steps, heads, KVL), jnp.bfloat16),
        in_specs=[
            smem,
            smem,
            pl.BlockSpec((1, height, entries), lambda r: (r, 0, 0)),
            pl.BlockSpec((1, height, KVL), lambda r: (r, 0, 0)),
            pl.BlockSpec((1, height, LANES), lambda r: (r, 0, 0)),
            pl.BlockSpec(memory_space=pl.ANY),
        ],
        out_specs=pl.BlockSpec((1, steps, heads, KVL), lambda r: (r, 0, 0, 0)),
        scratch_shapes=[
            pltpu.VMEM(arrived.shape, jnp.bfloat16),
            pltpu.VMEM((blocks * positions, entries), jnp.bfloat16),
            pltpu.SemaphoreType.DMA((arrived.shape[0],)),
        ],
        compiler_params=pltpu.CompilerParams(vmem_limit_bytes=60 * 1024 * 1024),
        name="attention",
    )(block_table, lengths, rows, partial, stats, arrived)


def local(
    queries,
    cache_pool,
    mig_block,
    block_table,
    lengths,
    hidden_states,
    routes,
    route_weight,
    w_gate,
    w_up,
    w_down,
):
    n = lax.axis_size("ep")
    split = FF // w_gate.shape[2]
    experts = n // split
    tokens = hidden_states.shape[0]
    ids = jnp.arange(experts, dtype=jnp.int32)
    matches = routes[:, :, None] == ids[None, None, :]
    hit = jnp.any(matches, axis=1)
    weight = jnp.sum(jnp.where(matches, route_weight[:, :, None], jnp.zeros((), jnp.bfloat16)), axis=1)
    order = jnp.arange(tokens)
    earlier = order[None, :] < order[:, None]
    rank = jnp.sum((earlier[:, :, None] & hit[None, :, :]).astype(jnp.int32), axis=1)
    slots = jnp.arange(SLOT)
    chosen = hit[:, :, None] & (rank[:, :, None] == slots)
    quarters = jnp.arange(QUARTERS)
    same = quarters[:, None] == quarters[None, :]
    wide = experts * QUARTERS * SLOT
    both = same[:, None, None, :, None] & chosen[None, :, :, None, :]
    combine = jnp.where(
        both, weight[None, :, :, None, None], jnp.zeros((), jnp.bfloat16)
    ).reshape(QUARTERS, tokens, wide)
    pick = both.astype(jnp.bfloat16).reshape(QUARTERS, tokens, wide).swapaxes(1, 2)
    arrived, moe_out, rows, partial, stats = exchange(
        cache_pool,
        mig_block,
        hidden_states,
        pick,
        combine,
        w_gate,
        w_up,
        w_down,
        block_table,
        lengths,
        queries.swapaxes(2, 3),
        n,
        split,
    )
    attn_out = attention(
        block_table,
        lengths,
        rows,
        partial,
        stats,
        arrived,
        cache_pool.shape[0],
        cache_pool.shape[1],
        queries.shape[1],
    )
    return attn_out, moe_out


def solution(mesh):
    placed = (
        P(("group", "ep"), None, None, None),
        P(("group", "ep"), None, None),
        P(("group", "ep"), None),
        P(("group", "ep"), None),
        P(("group", "ep")),
        P(("group", "ep"), None),
        P(("group", "ep"), None),
        P(("group", "ep"), None),
        P("ep", None, None),
        P("ep", None, None),
        P("ep", None, None),
    )
    return jax.shard_map(
        local,
        mesh=mesh,
        in_specs=placed,
        out_specs=(P(("group", "ep"), None, None, None), P(("group", "ep"), None)),
        check_vma=False,
    )
```

```python
import functools
import math

import jax
import jax.numpy as jnp
from jax import lax
from jax.experimental import pallas as pl
from jax.experimental.pallas import tpu as pltpu
from jax.sharding import PartitionSpec as P

KVL = 512
FF = 2048
SLOT = 4
QUARTERS = 4
LANES = 128
MESH = pl.DeviceIdType.MESH

softmax_scale = 0.1353
score_factor = softmax_scale * math.log2(math.e)
W1, W2 = 4, 12


def send(src, dst, send_sem, recv_sem, target):
    return pltpu.make_async_remote_copy(
        src_ref=src,
        dst_ref=dst,
        send_sem=send_sem,
        recv_sem=recv_sem,
        device_id={"ep": target},
        device_id_type=MESH,
    )


def spread(quarter, rows, cols, transposed):
    shape = (cols, rows) if transposed else (rows, cols)
    flat = lax.broadcasted_iota(jnp.int32, shape, 1 if transposed else 0)
    wide = lax.broadcasted_iota(jnp.int32, shape, 0 if transposed else 1)
    match = flat + (flat >> 2) * 12 + quarter * SLOT == wide
    return jnp.where(match, 1.0, 0.0).astype(jnp.bfloat16)


def exchange_kernel(
    n,
    split,
    mig_ref,
    pool_ref,
    hidden_ref,
    routes_ref,
    weight_ref,
    gate_ref,
    up_ref,
    down_ref,
    table_ref,
    lengths_ref,
    queries_ref,
    arrived_ref,
    moe_ref,
    rows_ref,
    partial_ref,
    stats_ref,
    pool_v,
    outgoing,
    gate_v,
    up_v,
    down_v,
    token_out,
    token_in,
    gathered,
    part_out,
    part_in,
    back_out,
    back_in,
    queries_v,
    rows_v,
    keys,
    bias,
    partial_v,
    stats_v,
    load_sem,
    mig_send,
    mig_recv,
    token_send,
    token_recv,
    gather_send,
    gather_recv,
    part_send,
    part_recv,
    back_send,
    back_recv,
    store_sem,
):
    me = lax.axis_index("ep")
    planes = n // split
    plane, place = me // split, me % split
    own_blocks = pool_ref.shape[0]
    width = hidden_ref.shape[1] // QUARTERS
    chunk = planes * SLOT
    wide = planes * SLOT * QUARTERS

    barrier = pltpu.get_barrier_semaphore()

    def greet(k, carry):
        pl.semaphore_signal(
            barrier, inc=1, device_id={"ep": (me + k) % n}, device_id_type=MESH
        )
        return carry

    lax.fori_loop(1, n, greet, 0)

    loads = [
        pltpu.make_async_copy(pool_ref, pool_v, load_sem.at[0]),
        pltpu.make_async_copy(gate_ref, gate_v, load_sem.at[1]),
        pltpu.make_async_copy(up_ref, up_v, load_sem.at[2]),
        pltpu.make_async_copy(down_ref, down_v, load_sem.at[3]),
        pltpu.make_async_copy(queries_ref, queries_v, load_sem.at[4]),
    ]
    loads[0].start()

    tokens = hidden_ref.shape[0]
    place_row = lax.broadcasted_iota(jnp.int32, (wide, tokens), 0)
    expert, row_quarter, slot = place_row >> 4, (place_row >> 2) & 3, place_row & 3
    hit = jnp.zeros((wide, tokens), jnp.float32)
    weight = jnp.zeros((wide, tokens), jnp.float32)
    weights = weight_ref[...].astype(jnp.float32)
    for k in range(routes_ref.shape[0]):
        same = routes_ref[k : k + 1, :] == expert
        hit = jnp.where(same, 1.0, hit)
        weight = jnp.where(same, weights[k : k + 1, :], weight)
    earlier = jnp.where(
        lax.broadcasted_iota(jnp.int32, (tokens, tokens), 0)
        < lax.broadcasted_iota(jnp.int32, (tokens, tokens), 1),
        1.0,
        0.0,
    )
    rank = jnp.dot(
        hit.astype(jnp.bfloat16), earlier.astype(jnp.bfloat16), preferred_element_type=jnp.float32
    )
    hit = jnp.where(rank == slot.astype(jnp.float32), hit, 0.0)
    weight = weight * hit

    def of_quarter(q, values):
        return jnp.where(row_quarter == q, values, 0.0).astype(jnp.bfloat16)

    messages = jnp.zeros((wide, width), jnp.float32)
    for q in range(QUARTERS):
        messages += jnp.dot(
            of_quarter(q, hit),
            hidden_ref[:, q * width : (q + 1) * width],
            preferred_element_type=jnp.float32,
        )
    token_out[...] = messages.astype(jnp.bfloat16).reshape(token_out.shape)
    token_in[plane] = token_out[plane]

    pl.semaphore_wait(barrier, n - 1)

    def token_copy(k):
        other = (plane + k) % planes
        return send(
            token_out.at[other],
            token_in.at[plane],
            token_send.at[k],
            token_recv.at[plane],
            other * split + place,
        )

    for k in range(1, planes):
        token_copy(k).start()

    loads[0].wait()
    for load in loads[1:]:
        load.start()

    def partner(k):
        flips = n - (k * 11) % n
        result = me
        for bit in range(n.bit_length() - 1):
            power = 2**bit
            flip = (flips // power) % 2
            held = (me // power) % 2
            result = result + flip * (1 - 2 * held) * power
        return result

    def mig_copy(k):
        return send(
            outgoing.at[k], arrived_ref.at[me], mig_send.at[k], mig_recv.at[me], partner(k)
        )

    def mig_start(k, carry):
        target = partner(k)
        block = jnp.minimum(mig_ref[0, target], own_blocks - 1)
        for c in range(KVL // LANES):
            outgoing[k, c * 64 : (c + 1) * 64, :] = pool_v[
                block, :, c * LANES : (c + 1) * LANES
            ]
        tail = pool_v[block, :, KVL:]
        outgoing[k, 256:288, :] = jnp.concatenate([tail[:32], tail[32:]], axis=1)
        mig_copy(k).start()
        return carry

    requests, blocks = table_ref.shape
    positions = pool_ref.shape[1]
    steps = queries_ref.shape[1]
    heads = queries_ref.shape[3]

    def kept_part(request, carry):
        length = lengths_ref[request]
        lane = lax.broadcasted_iota(jnp.int32, (1, positions), 1)
        for b in range(blocks):
            entry = table_ref[request, b]
            span = slice(b * positions, (b + 1) * positions)
            keys[span, :] = pool_v[jnp.minimum(entry, own_blocks - 1)]
            limit = jnp.where(entry < own_blocks, length - b * positions, 0)
            bias[:, span] = jnp.where(lane < limit, 0.0, -1e30)
        for step in range(steps):
            rows_v[request, step * heads : (step + 1) * heads, :] = queries_v[request, step].T
        scores = (
            lax.dot_general(
                rows_v[request],
                keys[...],
                (((1,), (1,)), ((), ())),
                preferred_element_type=jnp.float32,
            )
            * score_factor
            + bias[...]
        )
        row_max = jnp.max(scores, axis=1, keepdims=True)
        raised = jnp.exp2(scores - row_max)
        total = jnp.sum(raised, axis=1, keepdims=True)
        partial_v[request] = jnp.dot(
            raised.astype(jnp.bfloat16), keys[:, :KVL], preferred_element_type=jnp.float32
        )
        lane = lax.broadcasted_iota(jnp.int32, (steps * heads, LANES), 1)
        stats_v[request] = jnp.where(lane == 0, row_max, total)
        return carry

    stores = [
        pltpu.make_async_copy(rows_v, rows_ref, store_sem.at[0]),
        pltpu.make_async_copy(partial_v, partial_ref, store_sem.at[1]),
        pltpu.make_async_copy(stats_v, stats_ref, store_sem.at[2]),
    ]

    first, second = 1 + (n - 1) * W1 // 31, 1 + (n - 1) * W2 // 31
    lax.fori_loop(1, first, mig_start, 0)

    for k in range(1, planes):
        other = (plane + k) % planes
        send(
            token_out.at[k], token_in.at[other], token_send.at[k], token_recv.at[other], me
        ).wait_recv()
    arrived_tokens = token_in[...].reshape(wide, width)
    for q in range(QUARTERS):
        gathered[place, :, q * width : (q + 1) * width] = jnp.dot(
            spread(q, chunk, wide, False),
            arrived_tokens,
            preferred_element_type=jnp.float32,
        ).astype(jnp.bfloat16)

    def gather_copy(k):
        other = (place + k) % split
        return send(
            gathered.at[place],
            gathered.at[place],
            gather_send.at[k],
            gather_recv.at[place],
            plane * split + other,
        )

    for k in range(1, split):
        gather_copy(k).start()

    lax.fori_loop(first, second, mig_start, 0)

    for load in loads[1:]:
        load.wait()
    lax.fori_loop(0, requests // 2, kept_part, 0)
    for k in range(1, split):
        other = (place + k) % split
        send(
            gathered.at[place],
            gathered.at[other],
            gather_send.at[k],
            gather_recv.at[other],
            me,
        ).wait_recv()

    rows = gathered[...].reshape(split * chunk, gathered.shape[2])
    gate_act = jnp.dot(rows, gate_v[0], preferred_element_type=jnp.float32)
    up_act = jnp.dot(rows, up_v[0], preferred_element_type=jnp.float32)
    activation = (gate_act / (1.0 + jnp.exp(-gate_act)) * up_act).astype(jnp.bfloat16)
    for q in range(QUARTERS):
        columns = slice(q * width, (q + 1) * width)
        part_out[:, :, columns] = (
            jnp.dot(activation, down_v[0, :, columns], preferred_element_type=jnp.float32)
            .astype(jnp.bfloat16)
            .reshape(split, chunk, width)
        )

    def part_copy(k):
        other = (place + k) % split
        return send(
            part_out.at[other],
            part_in.at[place],
            part_send.at[k],
            part_recv.at[place],
            plane * split + other,
        )

    for k in range(1, split):
        part_copy(k).start()
    part_in[place] = part_out[place]

    lax.fori_loop(second, n, mig_start, 0)
    lax.fori_loop(requests // 2, requests, kept_part, 0)
    for store in stores:
        store.start()

    for k in range(1, split):
        other = (place + k) % split
        send(
            part_out.at[other], part_in.at[other], part_send.at[k], part_recv.at[other], me
        ).wait_recv()
    messages = jnp.zeros((wide, width), jnp.float32)
    for q in range(QUARTERS):
        columns = slice(q * width, (q + 1) * width)
        total = part_in[0, :, columns].astype(jnp.float32)
        for p in range(1, split):
            total += part_in[p, :, columns].astype(jnp.float32)
        messages += jnp.dot(
            spread(q, chunk, wide, True),
            total.astype(jnp.bfloat16),
            preferred_element_type=jnp.float32,
        )
    back_out[...] = messages.astype(jnp.bfloat16).reshape(back_out.shape)
    back_in[plane] = back_out[plane]

    def back_copy(k):
        other = (plane + k) % planes
        return send(
            back_out.at[other],
            back_in.at[plane],
            back_send.at[k],
            back_recv.at[plane],
            other * split + place,
        )

    for k in range(1, planes):
        back_copy(k).start()
    for k in range(1, planes):
        other = (plane + k) % planes
        send(
            back_out.at[k], back_in.at[other], back_send.at[k], back_recv.at[other], me
        ).wait_recv()
    returned = back_in[...].reshape(wide, width)
    for q in range(QUARTERS):
        moe_ref[:, q * width : (q + 1) * width] = lax.dot_general(
            of_quarter(q, weight),
            returned,
            (((0,), (0,)), ((), ())),
            preferred_element_type=jnp.float32,
        ).astype(jnp.bfloat16)

    for k in range(1, planes):
        token_copy(k).wait_send()
        back_copy(k).wait_send()
    for k in range(1, split):
        gather_copy(k).wait_send()
        part_copy(k).wait_send()

    def mig_wait(k, carry):
        source = partner(k)
        send(
            outgoing.at[k], arrived_ref.at[source], mig_send.at[k], mig_recv.at[source], me
        ).wait_recv()
        mig_copy(k).wait_send()
        return carry

    for store in stores:
        store.wait()
    lax.fori_loop(1, n, mig_wait, 0)


def exchange(
    cache_pool,
    mig_block,
    hidden_states,
    routes,
    route_weight,
    w_gate,
    w_up,
    w_down,
    block_table,
    lengths,
    queries,
    n,
    split,
):
    blocks, positions, entries = cache_pool.shape
    tokens, model_width = hidden_states.shape
    packed = positions * entries // LANES
    requests, steps, _, heads = queries.shape
    height = steps * heads
    length = block_table.shape[1] * positions
    planes = n // split
    chunk = planes * SLOT
    width = model_width // QUARTERS
    any_space = pl.BlockSpec(memory_space=pl.ANY)
    vmem = pl.BlockSpec(memory_space=pltpu.VMEM)
    smem = pl.BlockSpec(memory_space=pltpu.SMEM)
    bf16 = jnp.bfloat16
    dma = pltpu.SemaphoreType.DMA
    return pl.pallas_call(
        functools.partial(exchange_kernel, n, split),
        out_shape=(
            jax.ShapeDtypeStruct((n, packed, LANES), bf16),
            jax.ShapeDtypeStruct((tokens, model_width), bf16),
            jax.ShapeDtypeStruct((requests, height, entries), bf16),
            jax.ShapeDtypeStruct((requests, height, KVL), jnp.float32),
            jax.ShapeDtypeStruct((requests, height, LANES), jnp.float32),
        ),
        in_specs=[
            smem,
            any_space,
            vmem,
            vmem,
            vmem,
            any_space,
            any_space,
            any_space,
            smem,
            smem,
            any_space,
        ],
        out_specs=(any_space, vmem, any_space, any_space, any_space),
        scratch_shapes=[
            pltpu.VMEM(cache_pool.shape, bf16),
            pltpu.VMEM((n, packed, LANES), bf16),
            pltpu.VMEM(w_gate.shape, bf16),
            pltpu.VMEM(w_up.shape, bf16),
            pltpu.VMEM(w_down.shape, bf16),
            pltpu.VMEM((planes, SLOT * QUARTERS, width), bf16),
            pltpu.VMEM((planes, SLOT * QUARTERS, width), bf16),
            pltpu.VMEM((split, chunk, model_width), bf16),
            pltpu.VMEM((split, chunk, model_width), bf16),
            pltpu.VMEM((split, chunk, model_width), bf16),
            pltpu.VMEM((planes, SLOT * QUARTERS, width), bf16),
            pltpu.VMEM((planes, SLOT * QUARTERS, width), bf16),
            pltpu.VMEM(queries.shape, bf16),
            pltpu.VMEM((requests, height, entries), bf16),
            pltpu.VMEM((length, entries), bf16),
            pltpu.VMEM((1, length), jnp.float32),
            pltpu.VMEM((requests, height, KVL), jnp.float32),
            pltpu.VMEM((requests, height, LANES), jnp.float32),
            dma((5,)),
            dma((n,)),
            dma((n,)),
            dma((planes,)),
            dma((planes,)),
            dma((split,)),
            dma((split,)),
            dma((split,)),
            dma((split,)),
            dma((planes,)),
            dma((planes,)),
            dma((3,)),
        ],
        compiler_params=pltpu.CompilerParams(
            collective_id=0, has_side_effects=True, vmem_limit_bytes=60 * 1024 * 1024
        ),
        name="exchange",
    )(
        mig_block,
        cache_pool,
        hidden_states,
        routes,
        route_weight,
        w_gate,
        w_up,
        w_down,
        block_table,
        lengths,
        queries,
    )


def attend_kernel(
    own_blocks,
    positions,
    sizes,
    table_ref,
    lengths_ref,
    moe_ref,
    rows_ref,
    partial_ref,
    stats_ref,
    arrived_ref,
    out_ref,
    moe_out_ref,
    fetched,
    keys,
    rows_v,
    partial_v,
    stats_v,
    out_v,
    sem,
    load_sem,
    store_sem,
):
    requests, steps, heads = out_v.shape[:3]
    half = positions // 2

    def fetch(source):
        return pltpu.make_async_copy(
            arrived_ref.at[source], fetched.at[source], sem.at[source]
        )

    def used_blocks(row):
        return (lengths_ref[row] + positions - 1) // positions

    def begin(row):
        def begin_block(b, carry):
            entry = table_ref[row, b]

            @pl.when(entry >= own_blocks)
            def _():
                fetch(entry - own_blocks).start()

            return carry

        lax.fori_loop(0, used_blocks(row), begin_block, 0)

    def load_parts(row):
        return [
            pltpu.make_async_copy(whole.at[row], held.at[row], load_sem.at[part, row])
            for part, (whole, held) in enumerate(
                ((rows_ref, rows_v), (stats_ref, stats_v), (partial_ref, partial_v))
            )
        ]

    def store_part(row):
        return pltpu.make_async_copy(out_v.at[row], out_ref.at[row], store_sem.at[row])

    for row in range(requests):
        begin(row)
        for load in load_parts(row):
            load.start()
    keys[...] = jnp.zeros_like(keys)
    moe_out_ref[...] = moe_ref[...]

    def one_request(request, carry):
        length = lengths_ref[request]
        used = used_blocks(request)

        def place_block(b, count):
            entry = table_ref[request, b]
            moved = entry >= own_blocks

            @pl.when(moved)
            def _():
                source = entry - own_blocks
                fetch(source).wait()
                start = pl.multiple_of(count * positions, positions)
                for c in range(KVL // LANES):
                    keys[pl.ds(start, positions), c * LANES : (c + 1) * LANES] = fetched[
                        source, c * positions : (c + 1) * positions, :
                    ]
                tail = fetched[source, KVL // LANES * positions :, :]
                keys[pl.ds(start, half), KVL:] = tail[:, :64]
                keys[pl.ds(start + half, half), KVL:] = tail[:, 64:]

            return count + moved.astype(jnp.int32)

        count = lax.fori_loop(0, used, place_block, 0)
        last_moved = table_ref[request, used - 1] >= own_blocks
        limit = count * positions - jnp.where(last_moved, used * positions - length, 0)
        for load in load_parts(request):
            load.wait()
        old_max = stats_v[request, :, 0:1]
        old_total = stats_v[request, :, 1:2]

        def finish(out, total):
            out_v[request] = (
                (out * (1.0 / total)).astype(jnp.bfloat16).reshape(steps, heads, KVL)
            )

        @pl.when(count == 0)
        def _():
            finish(partial_v[request], old_total)

        def attend(size):
            rows = size * positions
            scores = (
                lax.dot_general(
                    rows_v[request],
                    keys[:rows, :],
                    (((1,), (1,)), ((), ())),
                    preferred_element_type=jnp.float32,
                )
                * score_factor
            )
            where = lax.broadcasted_iota(jnp.int32, scores.shape, 1)
            scores = jnp.where(where < limit, scores, -1e30)
            row_max = jnp.maximum(jnp.max(scores, axis=1, keepdims=True), old_max)
            raised = jnp.exp2(scores - row_max)
            keep = jnp.exp2(old_max - row_max)
            total = jnp.sum(raised, axis=1, keepdims=True) + keep * old_total
            out = keep * partial_v[request] + jnp.dot(
                raised.astype(jnp.bfloat16),
                keys[:rows, :KVL],
                preferred_element_type=jnp.float32,
            )
            finish(out, total)

        low = 0
        for size in sizes:

            @pl.when((count > low) & (count <= size))
            def _():
                attend(size)

            low = size
        store_part(request).start()
        return carry

    lax.fori_loop(0, requests, one_request, 0)
    for row in range(requests):
        store_part(row).wait()


def attention(block_table, lengths, moe, rows, partial, stats, arrived, own_blocks, positions, steps):
    requests, height, entries = rows.shape
    blocks = block_table.shape[1]
    sizes = tuple(c for c in (2, 4, 6, 8, 12) if c < blocks) + (blocks,)
    smem = pl.BlockSpec(memory_space=pltpu.SMEM)
    vmem = pl.BlockSpec(memory_space=pltpu.VMEM)
    any_space = pl.BlockSpec(memory_space=pl.ANY)
    heads = height // steps
    out_shape = jax.ShapeDtypeStruct((requests, steps, heads, KVL), jnp.bfloat16)
    return pl.pallas_call(
        functools.partial(attend_kernel, own_blocks, positions, sizes),
        out_shape=(out_shape, jax.ShapeDtypeStruct(moe.shape, moe.dtype)),
        in_specs=[smem, smem, vmem, any_space, any_space, any_space, any_space],
        out_specs=(any_space, vmem),
        scratch_shapes=[
            pltpu.VMEM(arrived.shape, jnp.bfloat16),
            pltpu.VMEM((blocks * positions, entries), jnp.bfloat16),
            pltpu.VMEM(rows.shape, rows.dtype),
            pltpu.VMEM(partial.shape, partial.dtype),
            pltpu.VMEM(stats.shape, stats.dtype),
            pltpu.VMEM(out_shape.shape, out_shape.dtype),
            pltpu.SemaphoreType.DMA((arrived.shape[0],)),
            pltpu.SemaphoreType.DMA((3, requests)),
            pltpu.SemaphoreType.DMA((requests,)),
        ],
        compiler_params=pltpu.CompilerParams(vmem_limit_bytes=60 * 1024 * 1024),
        name="attention",
    )(block_table, lengths, moe, rows, partial, stats, arrived)


def local(
    queries,
    cache_pool,
    mig_block,
    block_table,
    lengths,
    hidden_states,
    routes,
    route_weight,
    w_gate,
    w_up,
    w_down,
):
    n = lax.axis_size("ep")
    split = FF // w_gate.shape[2]
    arrived, moe_out, rows, partial, stats = exchange(
        cache_pool,
        mig_block,
        hidden_states,
        routes.T,
        route_weight.T,
        w_gate,
        w_up,
        w_down,
        block_table,
        lengths,
        queries.swapaxes(2, 3),
        n,
        split,
    )
    return attention(
        block_table,
        lengths,
        moe_out,
        rows,
        partial,
        stats,
        arrived,
        cache_pool.shape[0],
        cache_pool.shape[1],
        queries.shape[1],
    )


def solution(mesh):
    placed = (
        P(("group", "ep"), None, None, None),
        P(("group", "ep"), None, None),
        P(("group", "ep"), None),
        P(("group", "ep"), None),
        P(("group", "ep")),
        P(("group", "ep"), None),
        P(("group", "ep"), None),
        P(("group", "ep"), None),
        P("ep", None, None),
        P("ep", None, None),
        P("ep", None, None),
    )
    return jax.shard_map(
        local,
        mesh=mesh,
        in_specs=placed,
        out_specs=(P(("group", "ep"), None, None, None), P(("group", "ep"), None)),
        check_vma=False,
    )
```

```python
import functools
import math

import jax
import jax.numpy as jnp
from jax import lax
from jax.experimental import pallas as pl
from jax.experimental.pallas import tpu as pltpu
from jax.sharding import PartitionSpec as P

KVL = 512
FF = 2048
SLOT = 4
QUARTERS = 4
LANES = 128
MESH = pl.DeviceIdType.MESH

softmax_scale = 0.1353
score_factor = softmax_scale * math.log2(math.e)
W1, W2 = 4, 12


def send(src, dst, send_sem, recv_sem, target):
    return pltpu.make_async_remote_copy(
        src_ref=src,
        dst_ref=dst,
        send_sem=send_sem,
        recv_sem=recv_sem,
        device_id={"ep": target},
        device_id_type=MESH,
    )


def spread(quarter, rows, cols, transposed):
    shape = (cols, rows) if transposed else (rows, cols)
    flat = lax.broadcasted_iota(jnp.int32, shape, 1 if transposed else 0)
    wide = lax.broadcasted_iota(jnp.int32, shape, 0 if transposed else 1)
    match = flat + (flat >> 2) * 12 + quarter * SLOT == wide
    return jnp.where(match, 1.0, 0.0).astype(jnp.bfloat16)


def exchange_kernel(
    n,
    split,
    mig_ref,
    pool_ref,
    hidden_ref,
    routes_ref,
    weight_ref,
    gate_ref,
    up_ref,
    down_ref,
    table_ref,
    lengths_ref,
    queries_ref,
    arrived_ref,
    moe_ref,
    rows_ref,
    partial_ref,
    stats_ref,
    pool_v,
    outgoing,
    gate_v,
    up_v,
    down_v,
    token_out,
    token_in,
    gathered,
    part_out,
    part_in,
    back_out,
    back_in,
    queries_v,
    rows_v,
    keys,
    bias,
    partial_v,
    stats_v,
    load_sem,
    mig_send,
    mig_recv,
    token_send,
    token_recv,
    gather_send,
    gather_recv,
    part_send,
    part_recv,
    back_send,
    back_recv,
    store_sem,
):
    me = lax.axis_index("ep")
    planes = n // split
    plane, place = me // split, me % split
    own_blocks = pool_ref.shape[0]
    width = hidden_ref.shape[1] // QUARTERS
    chunk = planes * SLOT
    wide = planes * SLOT * QUARTERS

    barrier = pltpu.get_barrier_semaphore()

    def greet(k, carry):
        pl.semaphore_signal(
            barrier, inc=1, device_id={"ep": (me + k) % n}, device_id_type=MESH
        )
        return carry

    lax.fori_loop(1, n, greet, 0)

    loads = [
        pltpu.make_async_copy(gate_ref, gate_v, load_sem.at[1]),
        pltpu.make_async_copy(up_ref, up_v, load_sem.at[2]),
        pltpu.make_async_copy(down_ref, down_v, load_sem.at[3]),
        pltpu.make_async_copy(queries_ref, queries_v, load_sem.at[4]),
    ]
    part = own_blocks // 4
    pool_loads = [
        pltpu.make_async_copy(
            pool_ref.at[pl.ds(c * part, part)], pool_v.at[pl.ds(c * part, part)], load_sem.at[5 + c]
        )
        for c in range(4)
    ]
    for load in pool_loads:
        load.start()

    tokens = hidden_ref.shape[0]
    place_row = lax.broadcasted_iota(jnp.int32, (wide, tokens), 0)
    expert, row_quarter, slot = place_row >> 4, (place_row >> 2) & 3, place_row & 3
    hit = jnp.zeros((wide, tokens), jnp.float32)
    weight = jnp.zeros((wide, tokens), jnp.float32)
    weights = weight_ref[...].astype(jnp.float32)
    for k in range(routes_ref.shape[0]):
        same = routes_ref[k : k + 1, :] == expert
        hit = jnp.where(same, 1.0, hit)
        weight = jnp.where(same, weights[k : k + 1, :], weight)
    earlier = jnp.where(
        lax.broadcasted_iota(jnp.int32, (tokens, tokens), 0)
        < lax.broadcasted_iota(jnp.int32, (tokens, tokens), 1),
        1.0,
        0.0,
    )
    rank = jnp.dot(
        hit.astype(jnp.bfloat16), earlier.astype(jnp.bfloat16), preferred_element_type=jnp.float32
    )
    hit = jnp.where(rank == slot.astype(jnp.float32), hit, 0.0)
    weight = weight * hit

    def of_quarter(q, values):
        return jnp.where(row_quarter == q, values, 0.0).astype(jnp.bfloat16)

    messages = jnp.zeros((wide, width), jnp.float32)
    for q in range(QUARTERS):
        messages += jnp.dot(
            of_quarter(q, hit),
            hidden_ref[:, q * width : (q + 1) * width],
            preferred_element_type=jnp.float32,
        )
    token_out[...] = messages.astype(jnp.bfloat16).reshape(token_out.shape)
    token_in[plane] = token_out[plane]

    pl.semaphore_wait(barrier, n - 1)

    def token_copy(k):
        other = (plane + k) % planes
        return send(
            token_out.at[other],
            token_in.at[plane],
            token_send.at[k],
            token_recv.at[plane],
            other * split + place,
        )

    for k in range(1, planes):
        token_copy(k).start()

    for load in pool_loads:
        load.wait()
    for load in loads:
        load.start()

    def partner(k):
        flips = n - (k * 11) % n
        result = me
        for bit in range(n.bit_length() - 1):
            power = 2**bit
            flip = (flips // power) % 2
            held = (me // power) % 2
            result = result + flip * (1 - 2 * held) * power
        return result

    def mig_copy(k):
        return send(
            outgoing.at[k], arrived_ref.at[me], mig_send.at[k], mig_recv.at[me], partner(k)
        )

    def mig_start(k, carry):
        target = partner(k)
        block = jnp.minimum(mig_ref[0, target], own_blocks - 1)
        for c in range(KVL // LANES):
            outgoing[k, c * 64 : (c + 1) * 64, :] = pool_v[
                block, :, c * LANES : (c + 1) * LANES
            ]
        tail = pool_v[block, :, KVL:]
        outgoing[k, 256:288, :] = jnp.concatenate([tail[:32], tail[32:]], axis=1)
        mig_copy(k).start()
        return carry

    requests, blocks = table_ref.shape
    positions = pool_ref.shape[1]
    steps = queries_ref.shape[1]
    heads = queries_ref.shape[3]

    def kept_part(request, carry):
        length = lengths_ref[request]
        lane = lax.broadcasted_iota(jnp.int32, (1, positions), 1)
        for b in range(blocks):
            entry = table_ref[request, b]
            span = slice(b * positions, (b + 1) * positions)
            keys[span, :] = pool_v[jnp.minimum(entry, own_blocks - 1)]
            limit = jnp.where(entry < own_blocks, length - b * positions, 0)
            bias[:, span] = jnp.where(lane < limit, 0.0, -1e30)
        for step in range(steps):
            rows_v[request, step * heads : (step + 1) * heads, :] = queries_v[request, step].T
        scores = (
            lax.dot_general(
                rows_v[request],
                keys[...],
                (((1,), (1,)), ((), ())),
                preferred_element_type=jnp.float32,
            )
            * score_factor
            + bias[...]
        )
        row_max = jnp.max(scores, axis=1, keepdims=True)
        raised = jnp.exp2(scores - row_max)
        total = jnp.sum(raised, axis=1, keepdims=True)
        partial_v[request] = jnp.dot(
            raised.astype(jnp.bfloat16), keys[:, :KVL], preferred_element_type=jnp.float32
        )
        lane = lax.broadcasted_iota(jnp.int32, (steps * heads, LANES), 1)
        stats_v[request] = jnp.where(lane == 0, row_max, total)
        return carry

    stores = [
        pltpu.make_async_copy(rows_v, rows_ref, store_sem.at[0]),
        pltpu.make_async_copy(partial_v, partial_ref, store_sem.at[1]),
        pltpu.make_async_copy(stats_v, stats_ref, store_sem.at[2]),
    ]

    first, second = 1 + (n - 1) * W1 // 31, 1 + (n - 1) * W2 // 31
    lax.fori_loop(1, first, mig_start, 0)

    for k in range(1, planes):
        other = (plane + k) % planes
        send(
            token_out.at[k], token_in.at[other], token_send.at[k], token_recv.at[other], me
        ).wait_recv()
    arrived_tokens = token_in[...].reshape(wide, width)
    for q in range(QUARTERS):
        gathered[place, :, q * width : (q + 1) * width] = jnp.dot(
            spread(q, chunk, wide, False),
            arrived_tokens,
            preferred_element_type=jnp.float32,
        ).astype(jnp.bfloat16)

    def gather_copy(k):
        other = (place + k) % split
        return send(
            gathered.at[place],
            gathered.at[place],
            gather_send.at[k],
            gather_recv.at[place],
            plane * split + other,
        )

    for k in range(1, split):
        gather_copy(k).start()

    lax.fori_loop(first, second, mig_start, 0)

    for load in loads:
        load.wait()
    lax.fori_loop(0, requests // 2, kept_part, 0)
    for k in range(1, split):
        other = (place + k) % split
        send(
            gathered.at[place],
            gathered.at[other],
            gather_send.at[k],
            gather_recv.at[other],
            me,
        ).wait_recv()

    rows = gathered[...].reshape(split * chunk, gathered.shape[2])
    gate_act = jnp.dot(rows, gate_v[0], preferred_element_type=jnp.float32)
    up_act = jnp.dot(rows, up_v[0], preferred_element_type=jnp.float32)
    activation = (gate_act / (1.0 + jnp.exp(-gate_act)) * up_act).astype(jnp.bfloat16)
    for q in range(QUARTERS):
        columns = slice(q * width, (q + 1) * width)
        part_out[:, :, columns] = (
            jnp.dot(activation, down_v[0, :, columns], preferred_element_type=jnp.float32)
            .astype(jnp.bfloat16)
            .reshape(split, chunk, width)
        )

    def part_copy(k):
        other = (place + k) % split
        return send(
            part_out.at[other],
            part_in.at[place],
            part_send.at[k],
            part_recv.at[place],
            plane * split + other,
        )

    for k in range(1, split):
        part_copy(k).start()
    part_in[place] = part_out[place]

    lax.fori_loop(second, n, mig_start, 0)
    lax.fori_loop(requests // 2, requests, kept_part, 0)
    for store in stores:
        store.start()

    for k in range(1, split):
        other = (place + k) % split
        send(
            part_out.at[other], part_in.at[other], part_send.at[k], part_recv.at[other], me
        ).wait_recv()
    messages = jnp.zeros((wide, width), jnp.float32)
    for q in range(QUARTERS):
        columns = slice(q * width, (q + 1) * width)
        total = part_in[0, :, columns].astype(jnp.float32)
        for p in range(1, split):
            total += part_in[p, :, columns].astype(jnp.float32)
        messages += jnp.dot(
            spread(q, chunk, wide, True),
            total.astype(jnp.bfloat16),
            preferred_element_type=jnp.float32,
        )
    back_out[...] = messages.astype(jnp.bfloat16).reshape(back_out.shape)
    back_in[plane] = back_out[plane]

    def back_copy(k):
        other = (plane + k) % planes
        return send(
            back_out.at[other],
            back_in.at[plane],
            back_send.at[k],
            back_recv.at[plane],
            other * split + place,
        )

    for k in range(1, planes):
        back_copy(k).start()
    for k in range(1, planes):
        other = (plane + k) % planes
        send(
            back_out.at[k], back_in.at[other], back_send.at[k], back_recv.at[other], me
        ).wait_recv()
    returned = back_in[...].reshape(wide, width)
    for q in range(QUARTERS):
        moe_ref[:, q * width : (q + 1) * width] = lax.dot_general(
            of_quarter(q, weight),
            returned,
            (((0,), (0,)), ((), ())),
            preferred_element_type=jnp.float32,
        ).astype(jnp.bfloat16)

    for k in range(1, planes):
        token_copy(k).wait_send()
        back_copy(k).wait_send()
    for k in range(1, split):
        gather_copy(k).wait_send()
        part_copy(k).wait_send()

    def mig_wait(k, carry):
        source = partner(k)
        send(
            outgoing.at[k], arrived_ref.at[source], mig_send.at[k], mig_recv.at[source], me
        ).wait_recv()
        mig_copy(k).wait_send()
        return carry

    for store in stores:
        store.wait()
    lax.fori_loop(1, n, mig_wait, 0)


def exchange(
    cache_pool,
    mig_block,
    hidden_states,
    routes,
    route_weight,
    w_gate,
    w_up,
    w_down,
    block_table,
    lengths,
    queries,
    n,
    split,
):
    blocks, positions, entries = cache_pool.shape
    tokens, model_width = hidden_states.shape
    packed = positions * entries // LANES
    requests, steps, _, heads = queries.shape
    height = steps * heads
    length = block_table.shape[1] * positions
    planes = n // split
    chunk = planes * SLOT
    width = model_width // QUARTERS
    any_space = pl.BlockSpec(memory_space=pl.ANY)
    vmem = pl.BlockSpec(memory_space=pltpu.VMEM)
    smem = pl.BlockSpec(memory_space=pltpu.SMEM)
    bf16 = jnp.bfloat16
    dma = pltpu.SemaphoreType.DMA
    return pl.pallas_call(
        functools.partial(exchange_kernel, n, split),
        out_shape=(
            jax.ShapeDtypeStruct((n, packed, LANES), bf16),
            jax.ShapeDtypeStruct((tokens, model_width), bf16),
            jax.ShapeDtypeStruct((requests, height, entries), bf16),
            jax.ShapeDtypeStruct((requests, height, KVL), jnp.float32),
            jax.ShapeDtypeStruct((requests, height, LANES), jnp.float32),
        ),
        in_specs=[
            smem,
            any_space,
            vmem,
            vmem,
            vmem,
            any_space,
            any_space,
            any_space,
            smem,
            smem,
            any_space,
        ],
        out_specs=(any_space, vmem, any_space, any_space, any_space),
        scratch_shapes=[
            pltpu.VMEM(cache_pool.shape, bf16),
            pltpu.VMEM((n, packed, LANES), bf16),
            pltpu.VMEM(w_gate.shape, bf16),
            pltpu.VMEM(w_up.shape, bf16),
            pltpu.VMEM(w_down.shape, bf16),
            pltpu.VMEM((planes, SLOT * QUARTERS, width), bf16),
            pltpu.VMEM((planes, SLOT * QUARTERS, width), bf16),
            pltpu.VMEM((split, chunk, model_width), bf16),
            pltpu.VMEM((split, chunk, model_width), bf16),
            pltpu.VMEM((split, chunk, model_width), bf16),
            pltpu.VMEM((planes, SLOT * QUARTERS, width), bf16),
            pltpu.VMEM((planes, SLOT * QUARTERS, width), bf16),
            pltpu.VMEM(queries.shape, bf16),
            pltpu.VMEM((requests, height, entries), bf16),
            pltpu.VMEM((length, entries), bf16),
            pltpu.VMEM((1, length), jnp.float32),
            pltpu.VMEM((requests, height, KVL), jnp.float32),
            pltpu.VMEM((requests, height, LANES), jnp.float32),
            dma((9,)),
            dma((n,)),
            dma((n,)),
            dma((planes,)),
            dma((planes,)),
            dma((split,)),
            dma((split,)),
            dma((split,)),
            dma((split,)),
            dma((planes,)),
            dma((planes,)),
            dma((3,)),
        ],
        compiler_params=pltpu.CompilerParams(
            collective_id=0, has_side_effects=True, vmem_limit_bytes=60 * 1024 * 1024
        ),
        name="exchange",
    )(
        mig_block,
        cache_pool,
        hidden_states,
        routes,
        route_weight,
        w_gate,
        w_up,
        w_down,
        block_table,
        lengths,
        queries,
    )


def attend_kernel(
    own_blocks,
    positions,
    sizes,
    table_ref,
    lengths_ref,
    moe_ref,
    rows_ref,
    partial_ref,
    stats_ref,
    arrived_ref,
    out_ref,
    moe_out_ref,
    fetched,
    keys,
    rows_v,
    partial_v,
    stats_v,
    out_v,
    sem,
    load_sem,
    store_sem,
):
    requests, steps, heads = out_v.shape[:3]
    half = positions // 2

    def fetch(source):
        return pltpu.make_async_copy(
            arrived_ref.at[source], fetched.at[source], sem.at[source]
        )

    def used_blocks(row):
        return (lengths_ref[row] + positions - 1) // positions

    def begin(row):
        def begin_block(b, carry):
            entry = table_ref[row, b]

            @pl.when(entry >= own_blocks)
            def _():
                fetch(entry - own_blocks).start()

            return carry

        lax.fori_loop(0, used_blocks(row), begin_block, 0)

    def load_parts(row):
        return [
            pltpu.make_async_copy(whole.at[row], held.at[row], load_sem.at[part, row])
            for part, (whole, held) in enumerate(
                ((rows_ref, rows_v), (stats_ref, stats_v), (partial_ref, partial_v))
            )
        ]

    def store_part(row):
        return pltpu.make_async_copy(out_v.at[row], out_ref.at[row], store_sem.at[row])

    for row in range(requests):
        begin(row)
        for load in load_parts(row):
            load.start()
    keys[...] = jnp.zeros_like(keys)
    moe_out_ref[...] = moe_ref[...]

    def one_request(request, carry):
        length = lengths_ref[request]
        used = used_blocks(request)

        def place_block(b, count):
            entry = table_ref[request, b]
            moved = entry >= own_blocks

            @pl.when(moved)
            def _():
                source = entry - own_blocks
                fetch(source).wait()
                start = pl.multiple_of(count * positions, positions)
                for c in range(KVL // LANES):
                    keys[pl.ds(start, positions), c * LANES : (c + 1) * LANES] = fetched[
                        source, c * positions : (c + 1) * positions, :
                    ]
                tail = fetched[source, KVL // LANES * positions :, :]
                keys[pl.ds(start, half), KVL:] = tail[:, :64]
                keys[pl.ds(start + half, half), KVL:] = tail[:, 64:]

            return count + moved.astype(jnp.int32)

        count = lax.fori_loop(0, used, place_block, 0)
        last_moved = table_ref[request, used - 1] >= own_blocks
        limit = count * positions - jnp.where(last_moved, used * positions - length, 0)
        for load in load_parts(request):
            load.wait()
        old_max = stats_v[request, :, 0:1]
        old_total = stats_v[request, :, 1:2]

        def finish(out, total):
            out_v[request] = (
                (out * (1.0 / total)).astype(jnp.bfloat16).reshape(steps, heads, KVL)
            )

        @pl.when(count == 0)
        def _():
            finish(partial_v[request], old_total)

        def attend(size):
            rows = size * positions
            scores = (
                lax.dot_general(
                    rows_v[request],
                    keys[:rows, :],
                    (((1,), (1,)), ((), ())),
                    preferred_element_type=jnp.float32,
                )
                * score_factor
            )
            where = lax.broadcasted_iota(jnp.int32, scores.shape, 1)
            scores = jnp.where(where < limit, scores, -1e30)
            row_max = jnp.maximum(jnp.max(scores, axis=1, keepdims=True), old_max)
            raised = jnp.exp2(scores - row_max)
            keep = jnp.exp2(old_max - row_max)
            total = jnp.sum(raised, axis=1, keepdims=True) + keep * old_total
            out = keep * partial_v[request] + jnp.dot(
                raised.astype(jnp.bfloat16),
                keys[:rows, :KVL],
                preferred_element_type=jnp.float32,
            )
            finish(out, total)

        low = 0
        for size in sizes:

            @pl.when((count > low) & (count <= size))
            def _():
                attend(size)

            low = size
        store_part(request).start()
        return carry

    lax.fori_loop(0, requests, one_request, 0)
    for row in range(requests):
        store_part(row).wait()


def attention(block_table, lengths, moe, rows, partial, stats, arrived, own_blocks, positions, steps):
    requests, height, entries = rows.shape
    blocks = block_table.shape[1]
    sizes = tuple(c for c in (2, 4, 6, 8, 12) if c < blocks) + (blocks,)
    smem = pl.BlockSpec(memory_space=pltpu.SMEM)
    vmem = pl.BlockSpec(memory_space=pltpu.VMEM)
    any_space = pl.BlockSpec(memory_space=pl.ANY)
    heads = height // steps
    out_shape = jax.ShapeDtypeStruct((requests, steps, heads, KVL), jnp.bfloat16)
    return pl.pallas_call(
        functools.partial(attend_kernel, own_blocks, positions, sizes),
        out_shape=(out_shape, jax.ShapeDtypeStruct(moe.shape, moe.dtype)),
        in_specs=[smem, smem, vmem, any_space, any_space, any_space, any_space],
        out_specs=(any_space, vmem),
        scratch_shapes=[
            pltpu.VMEM(arrived.shape, jnp.bfloat16),
            pltpu.VMEM((blocks * positions, entries), jnp.bfloat16),
            pltpu.VMEM(rows.shape, rows.dtype),
            pltpu.VMEM(partial.shape, partial.dtype),
            pltpu.VMEM(stats.shape, stats.dtype),
            pltpu.VMEM(out_shape.shape, out_shape.dtype),
            pltpu.SemaphoreType.DMA((arrived.shape[0],)),
            pltpu.SemaphoreType.DMA((3, requests)),
            pltpu.SemaphoreType.DMA((requests,)),
        ],
        compiler_params=pltpu.CompilerParams(vmem_limit_bytes=60 * 1024 * 1024),
        name="attention",
    )(block_table, lengths, moe, rows, partial, stats, arrived)


def local(
    queries,
    cache_pool,
    mig_block,
    block_table,
    lengths,
    hidden_states,
    routes,
    route_weight,
    w_gate,
    w_up,
    w_down,
):
    n = lax.axis_size("ep")
    split = FF // w_gate.shape[2]
    arrived, moe_out, rows, partial, stats = exchange(
        cache_pool,
        mig_block,
        hidden_states,
        routes.T,
        route_weight.T,
        w_gate,
        w_up,
        w_down,
        block_table,
        lengths,
        queries.swapaxes(2, 3),
        n,
        split,
    )
    return attention(
        block_table,
        lengths,
        moe_out,
        rows,
        partial,
        stats,
        arrived,
        cache_pool.shape[0],
        cache_pool.shape[1],
        queries.shape[1],
    )


def solution(mesh):
    placed = (
        P(("group", "ep"), None, None, None),
        P(("group", "ep"), None, None),
        P(("group", "ep"), None),
        P(("group", "ep"), None),
        P(("group", "ep")),
        P(("group", "ep"), None),
        P(("group", "ep"), None),
        P(("group", "ep"), None),
        P("ep", None, None),
        P("ep", None, None),
        P("ep", None, None),
    )
    return jax.shard_map(
        local,
        mesh=mesh,
        in_specs=placed,
        out_specs=(P(("group", "ep"), None, None, None), P(("group", "ep"), None)),
        check_vma=False,
    )
```
